256 devices in a mesh: dp: 4 (over x), ctx: 64 (over z, y, core).
Axes of the slice: x: 4, y: 4, z: 8, core: 2. Of those that a mesh axis runs over, the one named last changes fastest.
Arguments:
- q_proj: bfloat16 [4, 8192, 4096], P('dp', 'ctx'), may hold values from -6 to 6
- k_proj: bfloat16 [4, 8192, 4096], P('dp', 'ctx'), may hold values from -6 to 6
- v_proj: bfloat16 [4, 8192, 4096], P('dp', 'ctx'), may hold values from -6 to 6
- out_grad: bfloat16 [4, 8192, 4096], P('dp', 'ctx'), may hold values from -6 to 6
- filters: bfloat16 [16, 256], replicated, may hold values from -0.375 to 0.375
- reaches: int32 [16], replicated, may hold values from 128 to 256, as said below
Outputs:
- grad_q: bfloat16 [4, 8192, 4096], P('dp', 'ctx')
- grad_k: bfloat16 [4, 8192, 4096], P('dp', 'ctx')
- grad_v: bfloat16 [4, 8192, 4096], P('dp', 'ctx')
- grad_filters: float32 [16, 256], replicated
The draws below stay inside these ranges and needn't reach their ends.
Inputs may be any that keep to these rules, and one draw needn't show every extreme that they name: `reaches`: every reach is a multiple of 128, and at least one group has reach exactly 256.
All inputs are finite; a program needn't handle non-finite values.
Results may differ from the reference program's by a relative error of at most 0.0049.
Values may be sent and summed in bfloat16 or wider, within the bound.
No kernel may reach another device: no remote copies, remote signals or barrier semaphores. Data moves between devices by JAX's collectives and lax.ppermute only.
A program may use at most 64 MiB of HBM per device.

```python
import math
import jax
import jax.numpy as jnp
from jax import lax

GROUPS = 16
CHANNELS = 4096
TOKENS = 8192
BATCH = 4
RMAX = 256


def draw_reaches(key, part):
    key = jax.random.fold_in(key, 7)
    first_key, second_key = jax.random.split(key)
    units = RMAX // 128
    base = jax.random.randint(first_key, (GROUPS,), 1, units + 1)
    chosen = jax.random.randint(second_key, (), 0, GROUPS)
    picked = jnp.where(jnp.arange(GROUPS) == chosen, units, base)
    return (picked * 128).astype(jnp.int32)


def block_scale(own_key, extent, pieces, least, top_value):
    factor_of, own = 1.0, jax.random.fold_in(own_key, 6)
    for axis_at, blocks in pieces:
        steps = jnp.exp(jax.random.uniform(jax.random.fold_in(own, axis_at), (blocks,), jnp.float32, least / len(pieces), top_value / len(pieces)))
        factor_of = factor_of * jnp.repeat(steps, extent[axis_at] // blocks).reshape([-1 if axis == axis_at else 1 for axis in range(len(extent))])
    return factor_of


def scatter_about(key, dims, scale, limit, cuts=(), kind=jnp.bfloat16):
    values = scale * jax.random.normal(key, dims, jnp.float32)
    if cuts:
        values = values * block_scale(key, dims, cuts, -0.22, 0.18)
    return jnp.clip(values, -limit, limit).astype(kind)


def setup_inputs(seed: int = 0) -> dict:
    key_of = jax.random.split(jax.random.key(seed), 7)
    q_proj = scatter_about(key_of[0], (BATCH, TOKENS, CHANNELS), 1.0, 6.0, ((0, 4), (1, 64)))
    k_proj = scatter_about(key_of[1], (BATCH, TOKENS, CHANNELS), 1.0, 6.0, ((0, 4), (1, 64)))
    v_proj = scatter_about(key_of[2], (BATCH, TOKENS, CHANNELS), 1.0, 6.0, ((0, 4), (1, 64)))
    out_grad = scatter_about(key_of[3], (BATCH, TOKENS, CHANNELS), 1.0, 6.0, ((0, 4), (1, 64)))
    filters = scatter_about(key_of[4], (GROUPS, RMAX), RMAX ** -0.5, 0.375)
    reaches = draw_reaches(jax.random.fold_in(key_of[6], 71), 0)
    return dict(q_proj=q_proj, k_proj=k_proj, v_proj=v_proj, out_grad=out_grad, filters=filters, reaches=reaches)


def toeplitz_blocks(masked, count, block_size):
    width = masked.shape[1]
    lag_block = jnp.arange(count + 1, dtype=jnp.int32)[:, None, None]
    row_pos = jnp.arange(block_size, dtype=jnp.int32)[None, :, None]
    col_pos = jnp.arange(block_size, dtype=jnp.int32)[None, None, :]
    position = lag_block * block_size + row_pos - col_pos
    valid = (position >= 0) & (position < width)
    kernels = jnp.take(masked, jnp.clip(position, 0, width - 1), axis=1)
    kernels = jnp.where(valid[None], kernels, jnp.zeros((), masked.dtype))
    return jnp.transpose(kernels, (1, 0, 2, 3))

def diagonal_sums(corr):
    block_size = corr.shape[-1]
    leading = corr.shape[:-2]
    flipped = jnp.flip(corr, -1)
    padded = jnp.concatenate([flipped, jnp.zeros_like(flipped)], axis=-1)
    flattened = padded.reshape(leading + (2 * block_size * block_size,))[..., :block_size * (2 * block_size - 1)]
    return flattened.reshape(leading + (block_size, 2 * block_size - 1)).sum(axis=-2)

def fold_diagonals(corr):
    count = corr.shape[0]
    block_size = corr.shape[-1]
    diag_sums = diagonal_sums(corr)
    shifted = jnp.concatenate([jnp.zeros_like(diag_sums[..., :1]), diag_sums], axis=-1)
    lower = shifted[..., :block_size]
    upper = shifted[..., block_size:]
    empty = jnp.zeros_like(lower[:1])
    placed = jnp.concatenate([lower, empty], 0) + jnp.concatenate([empty, upper], 0)
    kept = jnp.moveaxis(placed[1:count], 0, -2)
    return kept.reshape(kept.shape[:-2] + ((count - 1) * block_size,))

def reference(q_proj, k_proj, v_proj, out_grad, filters, reaches):
    batch_n, seq_n, chan_n = q_proj.shape
    group_n, width = filters.shape
    group_width = chan_n // group_n
    block_size = 128
    block_n = seq_n // block_size
    count = width // block_size + 1
    lags = jnp.arange(width, dtype=jnp.int32)
    keep = lags[None, :] < reaches[:, None]
    masked = jnp.where(keep, filters, jnp.zeros((), filters.dtype))
    signal = (k_proj.astype(jnp.float32) * v_proj.astype(jnp.float32)).astype(jnp.bfloat16)
    dconv = (out_grad.astype(jnp.float32) * q_proj.astype(jnp.float32)).astype(jnp.bfloat16)
    kernels = toeplitz_blocks(masked, count - 1, block_size)

    def regroup(array):
        return array.reshape(batch_n, block_n, block_size, group_n, group_width).transpose(3, 0, 1, 2, 4)

    def per_group(items):
        kern, sig, dcv, gate, kpart, vpart, cotan = items
        kern32 = kern.astype(jnp.float32)
        sig32 = sig.astype(jnp.float32)
        dcv32 = dcv.astype(jnp.float32)
        conv = jnp.zeros_like(sig32)
        dsignal = jnp.zeros_like(sig32)
        corrs = []
        for lag_block in range(count):
            sig_shift = jnp.concatenate([jnp.zeros_like(sig32[:, :lag_block]), sig32[:, :block_n - lag_block]], axis=1)
            dcv_shift = jnp.concatenate([dcv32[:, lag_block:], jnp.zeros_like(dcv32[:, :lag_block])], axis=1)
            conv = conv + jnp.einsum('ab,nkbc->nkac', kern32[lag_block], sig_shift, precision=lax.Precision.HIGHEST)
            dsignal = dsignal + jnp.einsum('ab,nkac->nkbc', kern32[lag_block], dcv_shift, precision=lax.Precision.HIGHEST)
            corrs.append(jnp.einsum('nkac,nkbc->ab', dcv32, sig_shift, precision=lax.Precision.HIGHEST))
        grad_taps = fold_diagonals(jnp.stack(corrs))
        grad_gate = (cotan.astype(jnp.float32) * conv).astype(jnp.bfloat16)
        grad_kpart = (dsignal * vpart.astype(jnp.float32)).astype(jnp.bfloat16)
        grad_vpart = (dsignal * kpart.astype(jnp.float32)).astype(jnp.bfloat16)
        return (grad_gate, grad_kpart, grad_vpart, grad_taps)
    results = lax.map(per_group, (kernels.transpose(1, 0, 2, 3), regroup(signal), regroup(dconv), regroup(q_proj), regroup(k_proj), regroup(v_proj), regroup(out_grad)))

    def restore(array):
        return array.transpose(1, 2, 3, 0, 4).reshape(batch_n, seq_n, chan_n)
    scale = 1.0 / math.sqrt(batch_n * seq_n * group_width)
    grad_filters = results[3] * keep.astype(jnp.float32) * scale
    return (restore(results[0]), restore(results[1]), restore(results[2]), grad_filters)
```

```python
import math

import jax
import jax.numpy as jnp
from jax import lax
from jax.experimental import pallas as pl
from jax.experimental.pallas import tpu as pltpu
from jax.sharding import PartitionSpec as P

F32 = jnp.float32
BF16 = jnp.bfloat16
TOK = 128
GW = 256


def gate_product_kernel(side_ref, a_ref, b_ref, c_ref, d_ref, out_ref):
    @pl.when(side_ref[0] == 1)
    def _():
        out_ref[...] = (a_ref[...].astype(F32) * b_ref[...].astype(F32)).astype(BF16)

    @pl.when(side_ref[0] == 0)
    def _():
        out_ref[...] = (c_ref[...].astype(F32) * d_ref[...].astype(F32)).astype(BF16)


def gate_product(side, a, b, c, d, blocks):
    tok_n, chan_n = a.shape
    width = chan_n // blocks
    first = pl.BlockSpec((tok_n, width), lambda i, s: (0, i * s[0]))
    second = pl.BlockSpec((tok_n, width), lambda i, s: (0, i * (1 - s[0])))
    return pl.pallas_call(
        gate_product_kernel,
        out_shape=jax.ShapeDtypeStruct(a.shape, BF16),
        grid_spec=pltpu.PrefetchScalarGridSpec(
            num_scalar_prefetch=1,
            grid=(blocks,),
            in_specs=[first, first, second, second],
            out_specs=pl.BlockSpec((tok_n, width), lambda i, s: (0, i)),
        ),
        cost_estimate=pl.CostEstimate(flops=a.size, bytes_accessed=6 * a.size, transcendentals=0),
    )(side, a, b, c, d)


def toeplitz(edges, reaches, filters):
    group_n = filters.shape[0]
    shape = jax.ShapeDtypeStruct((group_n, TOK, 3 * TOK), BF16)
    step = 8
    block = pl.BlockSpec((step, TOK, 3 * TOK), lambda i: (i, 0, 0))
    smem = pl.BlockSpec(memory_space=pltpu.SMEM)

    def kernel(edge_ref, reach_ref, filt_ref, ahead_ref, back_ref):
        base = pl.program_id(0) * step
        row = lax.broadcasted_iota(jnp.int32, (TOK, TOK), 0)
        col = lax.broadcasted_iota(jnp.int32, (TOK, TOK), 1)
        upper = col >= row
        lag = lax.broadcasted_iota(jnp.int32, (1, 2 * TOK), 1)
        back1, back2 = edge_ref[0].astype(F32), edge_ref[1].astype(F32)
        ahead1, ahead2 = edge_ref[2].astype(F32), edge_ref[3].astype(F32)
        zero = jnp.zeros((TOK, TOK), F32)
        lines = filt_ref[...].astype(F32)
        for g in range(step):
            line = jnp.where(lag < reach_ref[base + g], lines[g : g + 1, :], 0.0)
            near, far = (
                pltpu.roll(
                    jnp.broadcast_to(part, (TOK, TOK)), 0, axis=1, stride=1, stride_axis=0
                )
                for part in (line[:, :TOK], line[:, TOK:])
            )
            w0 = jnp.where(upper, near, zero)
            w1 = jnp.where(upper, far, near)
            w2 = jnp.where(upper, zero, far)
            ahead_ref[g, :, :TOK] = w0.astype(BF16)
            ahead_ref[g, :, TOK : 2 * TOK] = (w1 * ahead1).astype(BF16)
            ahead_ref[g, :, 2 * TOK :] = (w2 * ahead2).astype(BF16)
            back_ref[g, :, :TOK] = w0.T.astype(BF16)
            back_ref[g, :, TOK : 2 * TOK] = (w1 * back1).T.astype(BF16)
            back_ref[g, :, 2 * TOK :] = (w2 * back2).T.astype(BF16)

    return pl.pallas_call(
        kernel,
        out_shape=[shape, shape],
        grid=(group_n // step,),
        in_specs=[smem, smem, pl.BlockSpec((step, 2 * TOK), lambda i: (i, 0))],
        out_specs=[block, block],
        cost_estimate=pl.CostEstimate(
            flops=8 * group_n * TOK * TOK, bytes_accessed=12 * group_n * TOK * TOK, transcendentals=0
        ),
    )(edges, reaches, filters)


def taps_kernel(scale, step, flag_ref, reach_ref, mine_p, mine_x, got_p, got_x, out_ref):
    base = pl.program_id(0) * step
    row = lax.broadcasted_iota(jnp.int32, (TOK, TOK), 0)
    col = lax.broadcasted_iota(jnp.int32, (TOK, TOK), 1)
    upper = col >= row
    sub = lax.broadcasted_iota(jnp.int32, (8, TOK), 0)
    lane = lax.broadcasted_iota(jnp.int32, (1, TOK), 1)
    near_ok, far_ok = flag_ref[1].astype(F32), flag_ref[2].astype(F32)

    def diagonals(tile):
        acc = tile[0:8, :]
        for k in range(1, TOK // 8):
            acc = acc + pltpu.roll(tile[8 * k : 8 * k + 8, :], TOK - 8 * k, axis=1)
        for bit in (1, 2, 4):
            acc = jnp.where((sub & bit) != 0, pltpu.roll(acc, TOK - bit, axis=1), acc)
        return jnp.sum(acc, axis=0, keepdims=True)

    def pair(a, b):
        return lax.dot_general(a, b, (((1,), (1,)), ((), ())), preferred_element_type=F32)

    def work(sig, sig_back, dcv, dcv_ahead):
        for g in range(step):
            at = slice(g * GW, (g + 1) * GW)
            c0 = pair(sig[:, at], dcv[:, at])
            c1 = pair(sig_back[:, at], dcv[:, at]) * near_ok
            c2 = pair(sig_back[:, at], dcv_ahead[:, at]) * far_ok
            low = diagonals(jnp.where(upper, c0, c1))
            high = diagonals(jnp.where(upper, c1, c2))
            reach = reach_ref[base + g]
            out_ref[g : g + 1, :TOK] = jnp.where(lane < reach, low * scale, 0.0)
            out_ref[g : g + 1, TOK:] = jnp.where(lane + TOK < reach, high * scale, 0.0)

    @pl.when(flag_ref[0] == 1)
    def _():
        work(mine_p, got_x, mine_x, got_p)

    @pl.when(flag_ref[0] == 0)
    def _():
        work(mine_x, got_p, mine_p, got_x)


def taps(scale, flags, reaches, mine_p, mine_x, got_p, got_x):
    group_n = reaches.shape[0]
    step = 8
    smem = pl.BlockSpec(memory_space=pltpu.SMEM)
    block = pl.BlockSpec((TOK, step * GW), lambda i: (0, i))

    def kernel(*refs):
        taps_kernel(scale, step, *refs)

    return pl.pallas_call(
        kernel,
        out_shape=jax.ShapeDtypeStruct((group_n, 2 * TOK), F32),
        grid=(group_n // step,),
        in_specs=[smem, smem] + [block] * 4,
        out_specs=pl.BlockSpec((step, 2 * TOK), lambda i: (i, 0)),
        cost_estimate=pl.CostEstimate(
            flops=6 * group_n * TOK * TOK * GW, bytes_accessed=8 * mine_p.size, transcendentals=0
        ),
    )(flags, reaches, mine_p, mine_x, got_p, got_x)


def grads_piece(flags, ahead, back, fields, gates, outs, first, count, step):
    tok_n, chan_n = gates[0].shape
    smem = pl.BlockSpec(memory_space=pltpu.SMEM)
    start = first // step
    cols = pl.BlockSpec((tok_n, step * GW), lambda i: (0, i + start))
    mats = pl.BlockSpec((step, TOK, 3 * TOK), lambda i: (i + start, 0, 0))

    def kernel(flag_ref, ahead_ref, back_ref, *refs):
        mine_p, mine_x, got_p, got_x, got2_p, got2_x, grad, kpart, vpart = refs[:9]
        gq, gk, gv = refs[-3:]

        def dot(a, b):
            return jnp.dot(a, b, preferred_element_type=F32)

        def work(sig, sig1, sig2, dcv, dcv1, dcv2):
            for g in range(step):
                at = slice(g * GW, (g + 1) * GW)
                conv = (
                    dot(back_ref[g, :, :TOK], sig[:, at])
                    + dot(back_ref[g, :, TOK : 2 * TOK], sig1[:, at])
                    + dot(back_ref[g, :, 2 * TOK :], sig2[:, at])
                )
                gq[:, at] = (grad[:, at].astype(F32) * conv).astype(BF16)
                dsig = (
                    dot(ahead_ref[g, :, :TOK], dcv[:, at])
                    + dot(ahead_ref[g, :, TOK : 2 * TOK], dcv1[:, at])
                    + dot(ahead_ref[g, :, 2 * TOK :], dcv2[:, at])
                )
                gk[:, at] = (dsig * vpart[:, at].astype(F32)).astype(BF16)
                gv[:, at] = (dsig * kpart[:, at].astype(F32)).astype(BF16)

        @pl.when(flag_ref[0] == 1)
        def _():
            work(mine_p, got_x, got2_x, mine_x, got_p, got2_p)

        @pl.when(flag_ref[0] == 0)
        def _():
            work(mine_x, got_p, got2_p, mine_p, got_x, got2_x)

    shape = jax.ShapeDtypeStruct((tok_n, chan_n), BF16)
    earlier = [] if outs is None else list(outs)
    part = count * TOK * GW
    return pl.pallas_call(
        kernel,
        out_shape=[shape] * 3,
        grid=(count // step,),
        in_specs=[smem, mats, mats] + [cols] * 9 + [pl.BlockSpec(memory_space=pl.ANY)] * len(earlier),
        out_specs=[cols] * 3,
        input_output_aliases={12 + i: i for i in range(len(earlier))},
        cost_estimate=pl.CostEstimate(
            flops=12 * part * TOK, bytes_accessed=27 * part, transcendentals=0
        ),
    )(flags, ahead, back, *fields, *gates, *earlier)


def body(q_proj, k_proj, v_proj, out_grad, filters, reaches):
    batch_n, tok_n, chan_n = q_proj.shape
    group_n = filters.shape[0]
    ctx_n, dp_n = lax.axis_size("ctx"), lax.axis_size("dp")
    scale = 1.0 / math.sqrt(batch_n * dp_n * tok_n * ctx_n * (chan_n // group_n))
    q, k, v, grad = (x.reshape(tok_n, chan_n) for x in (q_proj, k_proj, v_proj, out_grad))

    me = lax.axis_index("ctx")
    odd = (me & 1).astype(jnp.int32)
    flags = jnp.stack([odd, me > 0, (me > 0) & (me < ctx_n - 1)]).astype(jnp.int32)
    edges = jnp.stack([me > 0, me > 1, me < ctx_n - 1, me < ctx_n - 2]).astype(jnp.int32)

    across = [(i, (i + 1) % ctx_n if i & 1 else (i - 1) % ctx_n) for i in range(ctx_n)]
    within = [(i, i ^ 1) for i in range(ctx_n)]

    mine_p = gate_product(odd[None], k, v, grad, q, 8)
    got_p = lax.ppermute(mine_p, "ctx", across)
    mine_x = gate_product(odd[None], grad, q, k, v, 8)
    got_x = lax.ppermute(mine_x, "ctx", within)
    got2_p = lax.ppermute(got_x, "ctx", across)
    ahead, back = toeplitz(edges, reaches, filters)
    local = taps(scale, flags, reaches, mine_p, mine_x, got_p, got_x)
    got2_x = lax.ppermute(got_p, "ctx", within)

    def trade_ctx(x, mask):
        return x + lax.ppermute(x, "ctx", [(i, i ^ mask) for i in range(ctx_n)])

    def trade_dp(x, mask):
        route = [
            (d * ctx_n + i, (d ^ mask) * ctx_n + (i ^ 1)) for d in range(dp_n) for i in range(ctx_n)
        ]
        return x + lax.ppermute(x, ("dp", "ctx"), route)

    total = trade_ctx(local, 1)
    total = trade_dp(total, 1)
    total = trade_dp(total, 3)
    total = trade_ctx(total, 8 | 1)
    outs = None
    fields = (mine_p, mine_x, got_p, got_x, got2_p, got2_x)
    pieces = 4
    for at, mask in enumerate((16 | 1, 56 | 1, 2 | 1, 6 | 1)):
        total, fields = lax.optimization_barrier((total, fields))
        outs = grads_piece(
            flags, ahead, back, fields, (grad, k, v), outs,
            at * group_n // pieces, group_n // pieces, 2,
        )
        total = trade_ctx(total, mask)
        total, outs = lax.optimization_barrier((total, outs))
    shaped = [x.reshape(batch_n, tok_n, chan_n) for x in outs]
    return (*shaped, total)


def solution(mesh):
    block = P("dp", "ctx", None)
    return jax.shard_map(
        body,
        mesh=mesh,
        in_specs=(block, block, block, block, P(), P()),
        out_specs=(block, block, block, P()),
        check_vma=False,
    )
```

```python
import math

import jax
import jax.numpy as jnp
from jax import lax
from jax.experimental import pallas as pl
from jax.experimental.pallas import tpu as pltpu
from jax.sharding import PartitionSpec as P

F32 = jnp.float32
BF16 = jnp.bfloat16
TOK = 128
GW = 256


def whole():
    return pl.BlockSpec(memory_space=pltpu.VMEM)


def smem():
    return pl.BlockSpec(memory_space=pltpu.SMEM)


def params(mib):
    return pltpu.CompilerParams(vmem_limit_bytes=mib * 2**20)


def gate_product(me, a, b, c, d, chunks, flops):
    tok_n, chan_n = a.shape
    parts = 4
    rows = tok_n // parts
    width = chan_n // chunks

    def kernel(me_ref, a_ref, b_ref, c_ref, d_ref, *refs):
        outs, (left, right, sems) = refs[:chunks], refs[chunks:]

        def run(x_ref, y_ref):
            copies = []
            for i in range(parts):
                at = pl.ds(i * rows, rows)
                pair = (
                    pltpu.make_async_copy(x_ref.at[at], left.at[at], sems.at[0, i]),
                    pltpu.make_async_copy(y_ref.at[at], right.at[at], sems.at[1, i]),
                )
                for copy in pair:
                    copy.start()
                copies.append(pair)
            for i, pair in enumerate(copies):
                for copy in pair:
                    copy.wait()
                at = pl.ds(i * rows, rows)
                for j, out in enumerate(outs):
                    cols = pl.ds(j * width, width)
                    prod = left[at, cols].astype(F32) * right[at, cols].astype(F32)
                    out[at, :] = prod.astype(BF16)

        odd = (me_ref[0] & 1) == 1

        @pl.when(odd)
        def _():
            run(a_ref, b_ref)

        @pl.when(jnp.logical_not(odd))
        def _():
            run(c_ref, d_ref)

    fixed = (pltpu.with_memory_space_constraint(x, pltpu.HBM) for x in (a, b, c, d))
    return pl.pallas_call(
        kernel,
        out_shape=[jax.ShapeDtypeStruct((tok_n, width), BF16)] * chunks,
        in_specs=[smem()] + [pl.BlockSpec(memory_space=pltpu.HBM)] * 4,
        out_specs=[whole()] * chunks,
        scratch_shapes=[
            pltpu.VMEM((tok_n, chan_n), BF16),
            pltpu.VMEM((tok_n, chan_n), BF16),
            pltpu.SemaphoreType.DMA((2, parts)),
        ],
        compiler_params=params(8),
        cost_estimate=pl.CostEstimate(flops=flops, bytes_accessed=6 * a.size, transcendentals=0),
    )(me, *fixed)


def columns(chunks, g, group_n):
    each = group_n // len(chunks)
    at = g % each
    return chunks[g // each][:, at * GW : (at + 1) * GW]


def toeplitz(me, last, reaches, filters):
    group_n = filters.shape[0]
    shape = jax.ShapeDtypeStruct((group_n, TOK, 3 * TOK), BF16)

    def kernel(me_ref, reach_ref, filt_ref, ahead_ref, back_ref):
        row = lax.broadcasted_iota(jnp.int32, (TOK, TOK), 0)
        col = lax.broadcasted_iota(jnp.int32, (TOK, TOK), 1)
        upper = col >= row
        lag = lax.broadcasted_iota(jnp.int32, (1, 2 * TOK), 1)
        here = me_ref[0]
        back1, back2 = (here > 0).astype(F32), (here > 1).astype(F32)
        ahead1, ahead2 = (here < last).astype(F32), (here < last - 1).astype(F32)
        zero = jnp.zeros((TOK, TOK), F32)
        lines = filt_ref[...].astype(F32)
        for g in range(group_n):
            line = jnp.where(lag < reach_ref[g], lines[g : g + 1, :], 0.0)
            near, far = (
                pltpu.roll(
                    jnp.broadcast_to(part, (TOK, TOK)), 0, axis=1, stride=1, stride_axis=0
                )
                for part in (line[:, :TOK], line[:, TOK:])
            )
            w0 = jnp.where(upper, near, zero)
            w1 = jnp.where(upper, far, near)
            w2 = jnp.where(upper, zero, far)
            ahead_ref[g, :, :TOK] = w0.astype(BF16)
            ahead_ref[g, :, TOK : 2 * TOK] = (w1 * ahead1).astype(BF16)
            ahead_ref[g, :, 2 * TOK :] = (w2 * ahead2).astype(BF16)
            back_ref[g, :, :TOK] = w0.T.astype(BF16)
            back_ref[g, :, TOK : 2 * TOK] = (w1 * back1).T.astype(BF16)
            back_ref[g, :, 2 * TOK :] = (w2 * back2).T.astype(BF16)

    return pl.pallas_call(
        kernel,
        out_shape=[shape, shape],
        in_specs=[smem(), smem(), whole()],
        out_specs=[whole(), whole()],
        compiler_params=params(8),
        cost_estimate=pl.CostEstimate(
            flops=group_n * TOK, bytes_accessed=group_n * TOK, transcendentals=0
        ),
    )(me, reaches, filters)


def taps(scale, last, me, reaches, mine_p, mine_x, got_p, got_x, first, count):
    group_n = reaches.shape[0]
    fields = (mine_p, mine_x, got_p, got_x)
    sizes = [len(x) for x in fields]

    def kernel(me_ref, reach_ref, *refs):
        out_ref = refs[-1]
        split, at = [], 0
        for size in sizes:
            split.append(refs[at : at + size])
            at += size
        mine_p, mine_x, got_p, got_x = split
        row = lax.broadcasted_iota(jnp.int32, (TOK, TOK), 0)
        col = lax.broadcasted_iota(jnp.int32, (TOK, TOK), 1)
        upper = col >= row
        sub = lax.broadcasted_iota(jnp.int32, (8, TOK), 0)
        lane = lax.broadcasted_iota(jnp.int32, (1, TOK), 1)
        here = me_ref[0]
        near_ok = (here > 0).astype(F32)
        far_ok = ((here > 0) & (here < last)).astype(F32)

        def diagonals(tile):
            acc = tile[0:8, :]
            for k in range(1, TOK // 8):
                acc = acc + pltpu.roll(tile[8 * k : 8 * k + 8, :], TOK - 8 * k, axis=1)
            for bit in (1, 2, 4):
                acc = jnp.where((sub & bit) != 0, pltpu.roll(acc, TOK - bit, axis=1), acc)
            return jnp.sum(acc, axis=0, keepdims=True)

        def pair(a, b):
            return lax.dot_general(a, b, (((1,), (1,)), ((), ())), preferred_element_type=F32)

        def work(sig, sig_back, dcv, dcv_ahead):
            for i in range(count):
                here_s, back_s, here_d, ahead_d = (
                    columns(x, i, count) for x in (sig, sig_back, dcv, dcv_ahead)
                )
                c0 = pair(here_s, here_d)
                c1 = pair(back_s, here_d) * near_ok
                c2 = pair(back_s, ahead_d) * far_ok
                low = diagonals(jnp.where(upper, c0, c1))
                high = diagonals(jnp.where(upper, c1, c2))
                reach = reach_ref[first + i]
                out_ref[i : i + 1, :TOK] = jnp.where(lane < reach, low * scale, 0.0)
                out_ref[i : i + 1, TOK:] = jnp.where(lane + TOK < reach, high * scale, 0.0)

        odd = (here & 1) == 1

        @pl.when(odd)
        def _():
            work(mine_p, got_x, mine_x, got_p)

        @pl.when(jnp.logical_not(odd))
        def _():
            work(mine_x, got_p, mine_p, got_x)

    flat = [x for field in fields for x in field]
    return pl.pallas_call(
        kernel,
        out_shape=jax.ShapeDtypeStruct((count, 2 * TOK), F32),
        in_specs=[smem(), smem()] + [whole()] * len(flat),
        out_specs=whole(),
        compiler_params=params(8),
        cost_estimate=pl.CostEstimate(
            flops=count * TOK, bytes_accessed=count * TOK, transcendentals=0
        ),
    )(me, reaches, *flat)


def grads_piece(me, ahead, back, fields, gates, outs, first, count, step):
    tok_n, chan_n = gates[0].shape
    group_n = chan_n // GW
    start = first // step
    each = [group_n // len(x) for x in fields]
    fields = [x[first // n] for x, n in zip(fields, each)]
    cols = pl.BlockSpec((tok_n, step * GW), lambda i: (0, i + start))

    def kernel(me_ref, ahead_ref, back_ref, *refs):
        grad, kpart, vpart = refs[6:9]
        gq, gk, gv = refs[-3:]
        base = first + pl.program_id(0) * step

        def dot(a, b):
            return jnp.dot(a, b, preferred_element_type=F32)

        def cols_of(ref, offset, g):
            return ref[:, pl.ds(pl.multiple_of((base - offset + g) * GW, GW), GW)]

        def work(*order):
            for g in range(step):
                at = slice(g * GW, (g + 1) * GW)
                src = pl.ds(pl.multiple_of((base + g) * GW, GW), GW)
                sig, sig1, sig2, dcv, dcv1, dcv2 = (
                    cols_of(refs[i], first - first % each[i], g) for i in order
                )
                back_mat = back_ref[base + g]
                conv = (
                    dot(back_mat[:, :TOK], sig)
                    + dot(back_mat[:, TOK : 2 * TOK], sig1)
                    + dot(back_mat[:, 2 * TOK :], sig2)
                )
                gq[:, at] = (grad[:, src].astype(F32) * conv).astype(BF16)
                ahead_mat = ahead_ref[base + g]
                dsig = (
                    dot(ahead_mat[:, :TOK], dcv)
                    + dot(ahead_mat[:, TOK : 2 * TOK], dcv1)
                    + dot(ahead_mat[:, 2 * TOK :], dcv2)
                )
                gk[:, at] = (dsig * vpart[:, src].astype(F32)).astype(BF16)
                gv[:, at] = (dsig * kpart[:, src].astype(F32)).astype(BF16)

        odd = (me_ref[0] & 1) == 1

        @pl.when(odd)
        def _():
            work(0, 3, 5, 1, 2, 4)

        @pl.when(jnp.logical_not(odd))
        def _():
            work(1, 2, 4, 0, 3, 5)

    shape = jax.ShapeDtypeStruct((tok_n, chan_n), BF16)
    earlier = [] if outs is None else list(outs)
    part = count * TOK * GW
    return pl.pallas_call(
        kernel,
        out_shape=[shape] * 3,
        grid=(count // step,),
        in_specs=[smem()] + [whole()] * 11 + [pl.BlockSpec(memory_space=pl.ANY)] * len(earlier),
        out_specs=[cols] * 3,
        input_output_aliases={12 + i: i for i in range(len(earlier))},
        compiler_params=params(8),
        cost_estimate=pl.CostEstimate(
            flops=12 * part * TOK, bytes_accessed=27 * part, transcendentals=0
        ),
    )(me, ahead, back, *fields, *gates, *earlier)


def body(q_proj, k_proj, v_proj, out_grad, filters, reaches):
    batch_n, tok_n, chan_n = q_proj.shape
    group_n = filters.shape[0]
    ctx_n, dp_n = lax.axis_size("ctx"), lax.axis_size("dp")
    scale = 1.0 / math.sqrt(batch_n * dp_n * tok_n * ctx_n * (chan_n // group_n))
    q, k, v, grad = (x.reshape(tok_n, chan_n) for x in (q_proj, k_proj, v_proj, out_grad))

    me = lax.axis_index("ctx").astype(jnp.int32)[None]
    last = ctx_n - 1

    across = [(i, (i + 1) % ctx_n if i & 1 else (i - 1) % ctx_n) for i in range(ctx_n)]
    within = [(i, i ^ 1) for i in range(ctx_n)]

    def trade(chunks, route):
        return [lax.ppermute(x, "ctx", route) for x in chunks]

    p_n, x_n = 1, 2
    mine_p = gate_product(me, k, v, grad, q, p_n, 1)
    got_p = trade(mine_p, across)
    mine_p, me = lax.optimization_barrier((mine_p, me))
    mine_x = gate_product(me, grad, q, k, v, x_n, 10**9)
    got_x = [jnp.concatenate(trade(mine_x, within), axis=1)]
    got_x, me = lax.optimization_barrier((got_x, me))
    got2_p = trade(got_x, across)
    ahead, back = toeplitz(me, last, reaches, filters)
    ahead, me = lax.optimization_barrier((ahead, me))
    local, got2_x = [], []
    each = group_n // p_n
    for i in range(p_n):
        here = slice(i * x_n // p_n, (i + 1) * x_n // p_n)
        term = taps(
            scale, last, me, reaches, mine_p[i : i + 1], mine_x[here], got_p[i : i + 1], got_x,
            i * each, each,
        )
        term, got_p[i], me = lax.optimization_barrier((term, got_p[i], me))
        got2_x.append(lax.ppermute(got_p[i], "ctx", within))
        local.append(term)
    local = jnp.concatenate(local)

    def trade_ctx(x, mask):
        return x + lax.ppermute(x, "ctx", [(i, i ^ mask) for i in range(ctx_n)])

    def trade_dp(x, mask):
        route = [
            (d * ctx_n + i, (d ^ mask) * ctx_n + (i ^ 1)) for d in range(dp_n) for i in range(ctx_n)
        ]
        return x + lax.ppermute(x, ("dp", "ctx"), route)

    total = trade_ctx(local, 1)
    total = trade_dp(total, 1)
    total = trade_dp(total, 3)
    total = trade_ctx(total, 8 | 1)
    outs = None
    fields = (mine_p, mine_x, got_p, got_x, got2_p, got2_x)
    pieces = 4
    for at, mask in enumerate((16 | 1, 56 | 1, 2 | 1, 6 | 1)):
        total, fields = lax.optimization_barrier((total, fields))
        outs = grads_piece(
            me, ahead, back, fields, (grad, k, v), outs,
            at * group_n // pieces, group_n // pieces, 2,
        )
        total = trade_ctx(total, mask)
        total, outs = lax.optimization_barrier((total, outs))
    shaped = [x.reshape(batch_n, tok_n, chan_n) for x in outs]
    return (*shaped, total)


def solution(mesh):
    block = P("dp", "ctx", None)
    return jax.shard_map(
        body,
        mesh=mesh,
        in_specs=(block, block, block, block, P(), P()),
        out_specs=(block, block, block, P()),
        check_vma=False,
    )
```

```python
import math

import jax
import jax.numpy as jnp
from jax import lax
from jax.experimental import pallas as pl
from jax.experimental.pallas import tpu as pltpu
from jax.sharding import PartitionSpec as P

F32 = jnp.float32
BF16 = jnp.bfloat16
TOK = 128
GW = 256


def whole():
    return pl.BlockSpec(memory_space=pltpu.VMEM)


def smem():
    return pl.BlockSpec(memory_space=pltpu.SMEM)


def params(mib):
    return pltpu.CompilerParams(vmem_limit_bytes=mib * 2**20)


def gate_product(me, a, b, c, d, chunks, flops):
    tok_n, chan_n = a.shape
    parts = 4
    rows = tok_n // parts
    width = chan_n // chunks

    def kernel(me_ref, a_ref, b_ref, c_ref, d_ref, *refs):
        outs, (left, right, sems) = refs[:chunks], refs[chunks:]

        def run(x_ref, y_ref):
            copies = []
            for i in range(parts):
                at = pl.ds(i * rows, rows)
                pair = (
                    pltpu.make_async_copy(x_ref.at[at], left.at[at], sems.at[0, i]),
                    pltpu.make_async_copy(y_ref.at[at], right.at[at], sems.at[1, i]),
                )
                for copy in pair:
                    copy.start()
                copies.append(pair)
            for i, pair in enumerate(copies):
                for copy in pair:
                    copy.wait()
                at = pl.ds(i * rows, rows)
                for j, out in enumerate(outs):
                    cols = pl.ds(j * width, width)
                    prod = left[at, cols].astype(F32) * right[at, cols].astype(F32)
                    out[at, :] = prod.astype(BF16)

        odd = (me_ref[0] & 1) == 1

        @pl.when(odd)
        def _():
            run(a_ref, b_ref)

        @pl.when(jnp.logical_not(odd))
        def _():
            run(c_ref, d_ref)

    fixed = (pltpu.with_memory_space_constraint(x, pltpu.HBM) for x in (a, b, c, d))
    return pl.pallas_call(
        kernel,
        out_shape=[jax.ShapeDtypeStruct((tok_n, width), BF16)] * chunks,
        in_specs=[smem()] + [pl.BlockSpec(memory_space=pltpu.HBM)] * 4,
        out_specs=[whole()] * chunks,
        scratch_shapes=[
            pltpu.VMEM((tok_n, chan_n), BF16),
            pltpu.VMEM((tok_n, chan_n), BF16),
            pltpu.SemaphoreType.DMA((2, parts)),
        ],
        compiler_params=params(8),
        cost_estimate=pl.CostEstimate(flops=flops, bytes_accessed=6 * a.size, transcendentals=0),
    )(me, *fixed)


def columns(chunks, g):
    at = g * GW
    for chunk in chunks:
        if at < chunk.shape[1]:
            return chunk[:, at : at + GW]
        at -= chunk.shape[1]


def toeplitz(me, last, reaches, filters):
    group_n = filters.shape[0]
    shape = jax.ShapeDtypeStruct((group_n, TOK, 3 * TOK), BF16)

    def kernel(me_ref, reach_ref, filt_ref, ahead_ref, back_ref):
        row = lax.broadcasted_iota(jnp.int32, (TOK, TOK), 0)
        col = lax.broadcasted_iota(jnp.int32, (TOK, TOK), 1)
        upper = col >= row
        lag = lax.broadcasted_iota(jnp.int32, (1, 2 * TOK), 1)
        here = me_ref[0]
        back1, back2 = (here > 0).astype(F32), (here > 1).astype(F32)
        ahead1, ahead2 = (here < last).astype(F32), (here < last - 1).astype(F32)
        zero = jnp.zeros((TOK, TOK), F32)
        lines = filt_ref[...].astype(F32)
        for g in range(group_n):
            line = jnp.where(lag < reach_ref[g], lines[g : g + 1, :], 0.0)
            near, far = (
                pltpu.roll(
                    jnp.broadcast_to(part, (TOK, TOK)), 0, axis=1, stride=1, stride_axis=0
                )
                for part in (line[:, :TOK], line[:, TOK:])
            )
            w0 = jnp.where(upper, near, zero)
            w1 = jnp.where(upper, far, near)
            w2 = jnp.where(upper, zero, far)
            ahead_ref[g, :, :TOK] = w0.astype(BF16)
            ahead_ref[g, :, TOK : 2 * TOK] = (w1 * ahead1).astype(BF16)
            ahead_ref[g, :, 2 * TOK :] = (w2 * ahead2).astype(BF16)
            back_ref[g, :, :TOK] = w0.T.astype(BF16)
            back_ref[g, :, TOK : 2 * TOK] = (w1 * back1).T.astype(BF16)
            back_ref[g, :, 2 * TOK :] = (w2 * back2).T.astype(BF16)

    return pl.pallas_call(
        kernel,
        out_shape=[shape, shape],
        in_specs=[smem(), smem(), whole()],
        out_specs=[whole(), whole()],
        compiler_params=params(8),
        cost_estimate=pl.CostEstimate(
            flops=group_n * TOK, bytes_accessed=group_n * TOK, transcendentals=0
        ),
    )(me, reaches, filters)


def tile_sums(upper, tile):
    sub = lax.broadcasted_iota(jnp.int32, (8, TOK), 0)
    acc = tile[0:8, :]
    for k in range(1, TOK // 8):
        acc = acc + pltpu.roll(tile[8 * k : 8 * k + 8, :], TOK - 8 * k, axis=1)
    for bit in (1, 2, 4):
        acc = jnp.where((sub & bit) != 0, pltpu.roll(acc, TOK - bit, axis=1), acc)
    return jnp.sum(acc, axis=0, keepdims=True)


def upper_mask():
    row = lax.broadcasted_iota(jnp.int32, (TOK, TOK), 0)
    col = lax.broadcasted_iota(jnp.int32, (TOK, TOK), 1)
    return col >= row


def cross(a, b):
    return lax.dot_general(a, b, (((1,), (1,)), ((), ())), preferred_element_type=F32)


def taps_inside(scale, me, reaches, mine_p, mine_x, got_x):
    group_n = mine_p.shape[1] // GW
    x_n = len(mine_x)

    def kernel(me_ref, reach_ref, mine_p, got_x, *refs):
        mine_x, out_ref, weight_ref = refs[:x_n], refs[x_n], refs[x_n + 1]
        upper = upper_mask()
        lag = lax.broadcasted_iota(jnp.int32, (1, 2 * TOK), 1)
        for g in range(group_n):
            weight_ref[g : g + 1, :] = jnp.where(lag < reach_ref[g], scale, 0.0).astype(F32)

        @pl.when((me_ref[0] & 1) == 1)
        def _():
            for g in range(group_n):
                dcv = columns(mine_x, g)
                c0 = cross(columns([mine_p], g), dcv)
                c1 = cross(columns([got_x], g), dcv)
                out_ref[g : g + 1, :TOK] = tile_sums(upper, jnp.where(upper, c0, c1))
                out_ref[g : g + 1, TOK:] = tile_sums(upper, jnp.where(upper, c1, 0.0))

        @pl.when((me_ref[0] & 1) == 0)
        def _():
            for g in range(group_n):
                c0 = cross(columns(mine_x, g), columns([mine_p], g))
                out_ref[g : g + 1, :TOK] = tile_sums(upper, jnp.where(upper, c0, 0.0))
            out_ref[:, TOK:] = jnp.zeros((group_n, TOK), F32)

    return pl.pallas_call(
        kernel,
        out_shape=[jax.ShapeDtypeStruct((group_n, 2 * TOK), F32)] * 2,
        in_specs=[smem(), smem()] + [whole()] * (2 + x_n),
        out_specs=[whole(), whole()],
        compiler_params=params(8),
        cost_estimate=pl.CostEstimate(
            flops=group_n * TOK, bytes_accessed=group_n * TOK, transcendentals=0
        ),
    )(me, reaches, mine_p, got_x, *mine_x)


def taps(last, me, inside, weight, mine_p, got_p, got_x):
    group_n = inside.shape[0]
    half = group_n // 2

    def kernel(me_ref, in_ref, weight_ref, mine_p, got_p, got_x, out_ref):
        upper = upper_mask()
        here = me_ref[0]
        odd = (here & 1) == 1

        def at(ref, g):
            return columns([ref], g)

        def work(near, far, near_groups, ok):
            for g in range(group_n):
                c2 = cross(*far(g))
                if g in near_groups:
                    c1 = cross(*near(g))
                    out_ref[g : g + 1, :TOK] = tile_sums(upper, jnp.where(upper, 0.0, c1))
                    out_ref[g : g + 1, TOK:] = tile_sums(upper, jnp.where(upper, c1, c2))
                else:
                    out_ref[g : g + 1, TOK:] = tile_sums(upper, jnp.where(upper, 0.0, c2))
            none = slice(half, group_n) if 0 in near_groups else slice(0, half)
            out_ref[none, :TOK] = jnp.zeros((half, TOK), F32)
            out_ref[...] = (in_ref[...] + jnp.where(ok, out_ref[...], 0.0)) * weight_ref[...]

        @pl.when(odd)
        def _():
            work(
                lambda g: (at(mine_p, g), at(got_p, g)),
                lambda g: (at(got_x, g), at(got_p, g)),
                range(half, group_n),
                here < last,
            )

        @pl.when(jnp.logical_not(odd))
        def _():
            work(
                lambda g: (at(got_p, g), at(mine_p, g)),
                lambda g: (at(got_p, g), at(got_x, g)),
                range(half),
                here > 0,
            )

    return pl.pallas_call(
        kernel,
        out_shape=jax.ShapeDtypeStruct((group_n, 2 * TOK), F32),
        in_specs=[smem()] + [whole()] * 5,
        out_specs=whole(),
        compiler_params=params(8),
        cost_estimate=pl.CostEstimate(
            flops=group_n * TOK, bytes_accessed=group_n * TOK, transcendentals=0
        ),
    )(me, inside, weight, mine_p, got_p, got_x)


def grads_piece(me, ahead, back, fields, gates, outs, first, count, step):
    tok_n, chan_n = gates[0].shape
    group_n = chan_n // GW
    start = first // step
    each = [group_n // len(x) for x in fields]
    fields = [x[first // n] for x, n in zip(fields, each)]
    cols = pl.BlockSpec((tok_n, step * GW), lambda i: (0, i + start))

    def kernel(me_ref, ahead_ref, back_ref, *refs):
        grad, kpart, vpart = refs[6:9]
        gq, gk, gv = refs[-3:]
        base = first + pl.program_id(0) * step

        def dot(a, b):
            return jnp.dot(a, b, preferred_element_type=F32)

        def cols_of(ref, offset, g):
            return ref[:, pl.ds(pl.multiple_of((base - offset + g) * GW, GW), GW)]

        def work(*order):
            for g in range(step):
                at = slice(g * GW, (g + 1) * GW)
                src = pl.ds(pl.multiple_of((base + g) * GW, GW), GW)
                sig, sig1, sig2, dcv, dcv1, dcv2 = (
                    cols_of(refs[i], first - first % each[i], g) for i in order
                )
                conv = dot(back_ref[base + g], jnp.concatenate([sig, sig1, sig2], axis=0))
                gq[:, at] = (grad[:, src].astype(F32) * conv).astype(BF16)
                dsig = dot(ahead_ref[base + g], jnp.concatenate([dcv, dcv1, dcv2], axis=0))
                gk[:, at] = (dsig * vpart[:, src].astype(F32)).astype(BF16)
                gv[:, at] = (dsig * kpart[:, src].astype(F32)).astype(BF16)

        odd = (me_ref[0] & 1) == 1

        @pl.when(odd)
        def _():
            work(0, 3, 5, 1, 2, 4)

        @pl.when(jnp.logical_not(odd))
        def _():
            work(1, 2, 4, 0, 3, 5)

    shape = jax.ShapeDtypeStruct((tok_n, chan_n), BF16)
    earlier = [] if outs is None else list(outs)
    part = count * TOK * GW
    return pl.pallas_call(
        kernel,
        out_shape=[shape] * 3,
        grid=(count // step,),
        in_specs=[smem()] + [whole()] * 11 + [pl.BlockSpec(memory_space=pl.ANY)] * len(earlier),
        out_specs=[cols] * 3,
        input_output_aliases={12 + i: i for i in range(len(earlier))},
        compiler_params=params(8),
        cost_estimate=pl.CostEstimate(
            flops=12 * part * TOK, bytes_accessed=27 * part, transcendentals=0
        ),
    )(me, ahead, back, *fields, *gates, *earlier)


def body(q_proj, k_proj, v_proj, out_grad, filters, reaches):
    batch_n, tok_n, chan_n = q_proj.shape
    group_n = filters.shape[0]
    ctx_n, dp_n = lax.axis_size("ctx"), lax.axis_size("dp")
    scale = 1.0 / math.sqrt(batch_n * dp_n * tok_n * ctx_n * (chan_n // group_n))
    q, k, v, grad = (x.reshape(tok_n, chan_n) for x in (q_proj, k_proj, v_proj, out_grad))

    me = lax.axis_index("ctx").astype(jnp.int32)[None]
    last = ctx_n - 1

    across = [(i, (i + 1) % ctx_n if i & 1 else (i - 1) % ctx_n) for i in range(ctx_n)]
    within = [(i, i ^ 1) for i in range(ctx_n)]

    def trade(chunks, route):
        return [lax.ppermute(x, "ctx", route) for x in chunks]

    p_n, x_n = 1, 2
    mine_p = gate_product(me, k, v, grad, q, p_n, 1)
    got_p = trade(mine_p, across)
    mine_p, me = lax.optimization_barrier((mine_p, me))
    mine_x = gate_product(me, grad, q, k, v, x_n, 10**9)
    got_x = [jnp.concatenate(trade(mine_x, within), axis=1)]
    got_x, me = lax.optimization_barrier((got_x, me))
    got2_p = trade(got_x, across)
    ahead, back = toeplitz(me, last, reaches, filters)
    ahead, me = lax.optimization_barrier((ahead, me))
    inside, weight = taps_inside(scale, me, reaches, mine_p[0], mine_x, got_x[0])
    local = taps(last, me, inside, weight, mine_p[0], got_p[0], got_x[0])
    local, got_p = lax.optimization_barrier((local, got_p))
    got2_x = trade(got_p, within)

    def trade_ctx(x, mask):
        return x + lax.ppermute(x, "ctx", [(i, i ^ mask) for i in range(ctx_n)])

    def trade_dp(x, mask):
        route = [
            (d * ctx_n + i, (d ^ mask) * ctx_n + (i ^ 1)) for d in range(dp_n) for i in range(ctx_n)
        ]
        return x + lax.ppermute(x, ("dp", "ctx"), route)

    total = trade_dp(local, 1)
    total = trade_dp(total, 3)
    total = trade_ctx(total, 1)
    total = trade_ctx(total, 8 | 1)
    outs = None
    fields = (mine_p, mine_x, got_p, got_x, got2_p, got2_x)
    pieces = 4
    for at, mask in enumerate((16 | 1, 56 | 1, 2 | 1, 6 | 1)):
        total, fields = lax.optimization_barrier((total, fields))
        outs = grads_piece(
            me, ahead, back, fields, (grad, k, v), outs,
            at * group_n // pieces, group_n // pieces, 2,
        )
        total = trade_ctx(total, mask)
        total, outs = lax.optimization_barrier((total, outs))
    shaped = [x.reshape(batch_n, tok_n, chan_n) for x in outs]
    return (*shaped, total)


def solution(mesh):
    block = P("dp", "ctx", None)
    return jax.shard_map(
        body,
        mesh=mesh,
        in_specs=(block, block, block, block, P(), P()),
        out_specs=(block, block, block, P()),
        check_vma=False,
    )
```

```python
import math

import jax
import jax.numpy as jnp
from jax import lax
from jax.experimental import pallas as pl
from jax.experimental.pallas import tpu as pltpu
from jax.sharding import PartitionSpec as P

F32 = jnp.float32
BF16 = jnp.bfloat16
TOK = 128
GW = 256


def whole():
    return pl.BlockSpec(memory_space=pltpu.VMEM)


def smem():
    return pl.BlockSpec(memory_space=pltpu.SMEM)


def params(mib):
    return pltpu.CompilerParams(vmem_limit_bytes=mib * 2**20)


def gate_product(me, a, b, c, d, chunks, flops):
    tok_n, chan_n = a.shape
    parts = 4
    rows = tok_n // parts
    width = chan_n // chunks

    def kernel(me_ref, a_ref, b_ref, c_ref, d_ref, *refs):
        outs, (left, right, sems) = refs[:chunks], refs[chunks:]

        def run(x_ref, y_ref):
            copies = []
            for i in range(parts):
                at = pl.ds(i * rows, rows)
                pair = (
                    pltpu.make_async_copy(x_ref.at[at], left.at[at], sems.at[0, i]),
                    pltpu.make_async_copy(y_ref.at[at], right.at[at], sems.at[1, i]),
                )
                for copy in pair:
                    copy.start()
                copies.append(pair)
            for i, pair in enumerate(copies):
                for copy in pair:
                    copy.wait()
                at = pl.ds(i * rows, rows)
                for j, out in enumerate(outs):
                    cols = pl.ds(j * width, width)
                    prod = left[at, cols].astype(F32) * right[at, cols].astype(F32)
                    out[at, :] = prod.astype(BF16)

        odd = (me_ref[0] & 1) == 1

        @pl.when(odd)
        def _():
            run(a_ref, b_ref)

        @pl.when(jnp.logical_not(odd))
        def _():
            run(c_ref, d_ref)

    fixed = (pltpu.with_memory_space_constraint(x, pltpu.HBM) for x in (a, b, c, d))
    return pl.pallas_call(
        kernel,
        out_shape=[jax.ShapeDtypeStruct((tok_n, width), BF16)] * chunks,
        in_specs=[smem()] + [pl.BlockSpec(memory_space=pltpu.HBM)] * 4,
        out_specs=[whole()] * chunks,
        scratch_shapes=[
            pltpu.VMEM((tok_n, chan_n), BF16),
            pltpu.VMEM((tok_n, chan_n), BF16),
            pltpu.SemaphoreType.DMA((2, parts)),
        ],
        compiler_params=params(8),
        cost_estimate=pl.CostEstimate(flops=flops, bytes_accessed=6 * a.size, transcendentals=0),
    )(me, *fixed)


def columns(chunks, g):
    at = g * GW
    for chunk in chunks:
        if at < chunk.shape[1]:
            return chunk[:, at : at + GW]
        at -= chunk.shape[1]


def toeplitz(me, last, reaches, filters):
    group_n = filters.shape[0]
    shape = jax.ShapeDtypeStruct((group_n, TOK, 3 * TOK), BF16)

    def kernel(me_ref, reach_ref, filt_ref, ahead_ref, back_ref):
        row = lax.broadcasted_iota(jnp.int32, (TOK, TOK), 0)
        col = lax.broadcasted_iota(jnp.int32, (TOK, TOK), 1)
        upper = col >= row
        lag = lax.broadcasted_iota(jnp.int32, (1, 2 * TOK), 1)
        here = me_ref[0]
        back1, back2 = (here > 0).astype(F32), (here > 1).astype(F32)
        ahead1, ahead2 = (here < last).astype(F32), (here < last - 1).astype(F32)
        zero = jnp.zeros((TOK, TOK), F32)
        lines = filt_ref[...].astype(F32)
        for g in range(group_n):
            line = jnp.where(lag < reach_ref[g], lines[g : g + 1, :], 0.0)
            near, far = (
                pltpu.roll(
                    jnp.broadcast_to(part, (TOK, TOK)), 0, axis=1, stride=1, stride_axis=0
                )
                for part in (line[:, :TOK], line[:, TOK:])
            )
            w0 = jnp.where(upper, near, zero)
            w1 = jnp.where(upper, far, near)
            w2 = jnp.where(upper, zero, far)
            ahead_ref[g, :, :TOK] = w0.astype(BF16)
            ahead_ref[g, :, TOK : 2 * TOK] = (w1 * ahead1).astype(BF16)
            ahead_ref[g, :, 2 * TOK :] = (w2 * ahead2).astype(BF16)
            back_ref[g, :, :TOK] = w0.T.astype(BF16)
            back_ref[g, :, TOK : 2 * TOK] = (w1 * back1).T.astype(BF16)
            back_ref[g, :, 2 * TOK :] = (w2 * back2).T.astype(BF16)

    return pl.pallas_call(
        kernel,
        out_shape=[shape, shape],
        in_specs=[smem(), smem(), whole()],
        out_specs=[whole(), whole()],
        compiler_params=params(8),
        cost_estimate=pl.CostEstimate(
            flops=group_n * TOK, bytes_accessed=group_n * TOK, transcendentals=0
        ),
    )(me, reaches, filters)


def tile_sums(upper, tile):
    sub = lax.broadcasted_iota(jnp.int32, (8, TOK), 0)
    acc = tile[0:8, :]
    for k in range(1, TOK // 8):
        acc = acc + pltpu.roll(tile[8 * k : 8 * k + 8, :], TOK - 8 * k, axis=1)
    for bit in (1, 2, 4):
        acc = jnp.where((sub & bit) != 0, pltpu.roll(acc, TOK - bit, axis=1), acc)
    return jnp.sum(acc, axis=0, keepdims=True)


def upper_mask():
    row = lax.broadcasted_iota(jnp.int32, (TOK, TOK), 0)
    col = lax.broadcasted_iota(jnp.int32, (TOK, TOK), 1)
    return col >= row


def cross(a, b):
    return lax.dot_general(a, b, (((1,), (1,)), ((), ())), preferred_element_type=F32)


def taps_inside(scale, me, reaches, mine_p, mine_x, got_x):
    group_n = mine_p.shape[1] // GW
    x_n = len(mine_x)

    def kernel(me_ref, reach_ref, mine_p, got_x, *refs):
        mine_x, out_ref, weight_ref = refs[:x_n], refs[x_n], refs[x_n + 1]
        upper = upper_mask()
        lag = lax.broadcasted_iota(jnp.int32, (1, 2 * TOK), 1)
        for g in range(group_n):
            weight_ref[g : g + 1, :] = jnp.where(lag < reach_ref[g], scale, 0.0).astype(F32)

        @pl.when((me_ref[0] & 1) == 1)
        def _():
            for g in range(group_n):
                dcv = columns(mine_x, g)
                c0 = cross(columns([mine_p], g), dcv)
                c1 = cross(columns([got_x], g), dcv)
                out_ref[g : g + 1, :TOK] = tile_sums(upper, jnp.where(upper, c0, c1))
                out_ref[g : g + 1, TOK:] = tile_sums(upper, jnp.where(upper, c1, 0.0))

        @pl.when((me_ref[0] & 1) == 0)
        def _():
            for g in range(group_n):
                c0 = cross(columns(mine_x, g), columns([mine_p], g))
                out_ref[g : g + 1, :TOK] = tile_sums(upper, jnp.where(upper, c0, 0.0))
            out_ref[:, TOK:] = jnp.zeros((group_n, TOK), F32)

    return pl.pallas_call(
        kernel,
        out_shape=[jax.ShapeDtypeStruct((group_n, 2 * TOK), F32)] * 2,
        in_specs=[smem(), smem()] + [whole()] * (2 + x_n),
        out_specs=[whole(), whole()],
        compiler_params=params(8),
        cost_estimate=pl.CostEstimate(
            flops=group_n * TOK, bytes_accessed=group_n * TOK, transcendentals=0
        ),
    )(me, reaches, mine_p, got_x, *mine_x)


def taps(last, me, inside, weight, mine_p, got_p, got_x):
    group_n = inside.shape[0]
    half = group_n // 2

    def kernel(me_ref, in_ref, weight_ref, mine_p, got_p, got_x, out_ref):
        upper = upper_mask()
        here = me_ref[0]
        odd = (here & 1) == 1

        def at(ref, g):
            return columns([ref], g)

        def work(near, far, near_groups, ok):
            for g in range(group_n):
                c2 = cross(*far(g))
                if g in near_groups:
                    c1 = cross(*near(g))
                    out_ref[g : g + 1, :TOK] = tile_sums(upper, jnp.where(upper, 0.0, c1))
                    out_ref[g : g + 1, TOK:] = tile_sums(upper, jnp.where(upper, c1, c2))
                else:
                    out_ref[g : g + 1, TOK:] = tile_sums(upper, jnp.where(upper, 0.0, c2))
            none = slice(half, group_n) if 0 in near_groups else slice(0, half)
            out_ref[none, :TOK] = jnp.zeros((half, TOK), F32)
            out_ref[...] = (in_ref[...] + jnp.where(ok, out_ref[...], 0.0)) * weight_ref[...]

        @pl.when(odd)
        def _():
            work(
                lambda g: (at(mine_p, g), at(got_p, g)),
                lambda g: (at(got_x, g), at(got_p, g)),
                range(half, group_n),
                here < last,
            )

        @pl.when(jnp.logical_not(odd))
        def _():
            work(
                lambda g: (at(got_p, g), at(mine_p, g)),
                lambda g: (at(got_p, g), at(got_x, g)),
                range(half),
                here > 0,
            )

    return pl.pallas_call(
        kernel,
        out_shape=jax.ShapeDtypeStruct((group_n, 2 * TOK), F32),
        in_specs=[smem()] + [whole()] * 5,
        out_specs=whole(),
        compiler_params=params(8),
        cost_estimate=pl.CostEstimate(
            flops=group_n * TOK, bytes_accessed=group_n * TOK, transcendentals=0
        ),
    )(me, inside, weight, mine_p, got_p, got_x)


def grads_piece(me, ahead, back, fields, gates, outs, first, count, step):
    tok_n, chan_n = gates[0].shape
    group_n = chan_n // GW
    start = first // step
    each = [group_n // len(x) for x in fields]
    fields = [x[first // n] for x, n in zip(fields, each)]
    cols = pl.BlockSpec((tok_n, step * GW), lambda i: (0, i + start))

    def kernel(me_ref, ahead_ref, back_ref, *refs):
        grad, kpart, vpart = refs[6:9]
        gq, gk, gv = refs[-3:]
        base = first + pl.program_id(0) * step

        def dot(a, b):
            return jnp.dot(a, b, preferred_element_type=F32)

        def cols_of(ref, offset, g):
            return ref[:, pl.ds(pl.multiple_of((base - offset + g) * GW, GW), GW)]

        def work(*order):
            for g in range(step):
                at = slice(g * GW, (g + 1) * GW)
                src = pl.ds(pl.multiple_of((base + g) * GW, GW), GW)
                sig, sig1, sig2, dcv, dcv1, dcv2 = (
                    cols_of(refs[i], first - first % each[i], g) for i in order
                )
                conv = dot(back_ref[base + g], jnp.concatenate([sig, sig1, sig2], axis=0))
                gq[:, at] = (grad[:, src].astype(F32) * conv).astype(BF16)
                dsig = dot(ahead_ref[base + g], jnp.concatenate([dcv, dcv1, dcv2], axis=0))
                gk[:, at] = (dsig * vpart[:, src].astype(F32)).astype(BF16)
                gv[:, at] = (dsig * kpart[:, src].astype(F32)).astype(BF16)

        odd = (me_ref[0] & 1) == 1

        @pl.when(odd)
        def _():
            work(0, 3, 5, 1, 2, 4)

        @pl.when(jnp.logical_not(odd))
        def _():
            work(1, 2, 4, 0, 3, 5)

    shape = jax.ShapeDtypeStruct((tok_n, chan_n), BF16)
    earlier = [] if outs is None else list(outs)
    part = count * TOK * GW
    return pl.pallas_call(
        kernel,
        out_shape=[shape] * 3,
        grid=(count // step,),
        in_specs=[smem()] + [whole()] * 11 + [pl.BlockSpec(memory_space=pl.ANY)] * len(earlier),
        out_specs=[cols] * 3,
        input_output_aliases={12 + i: i for i in range(len(earlier))},
        compiler_params=params(8),
        cost_estimate=pl.CostEstimate(
            flops=12 * part * TOK, bytes_accessed=27 * part, transcendentals=0
        ),
    )(me, ahead, back, *fields, *gates, *earlier)


def body(q_proj, k_proj, v_proj, out_grad, filters, reaches):
    batch_n, tok_n, chan_n = q_proj.shape
    group_n = filters.shape[0]
    ctx_n, dp_n = lax.axis_size("ctx"), lax.axis_size("dp")
    scale = 1.0 / math.sqrt(batch_n * dp_n * tok_n * ctx_n * (chan_n // group_n))
    q, k, v, grad = (x.reshape(tok_n, chan_n) for x in (q_proj, k_proj, v_proj, out_grad))

    me = lax.axis_index("ctx").astype(jnp.int32)[None]
    last = ctx_n - 1

    def partner(d, i):
        if i in (0, last):
            return (d ^ 1) * ctx_n + i
        return d * ctx_n + (i + 1 if i & 1 else i - 1)

    across = [(d * ctx_n + i, partner(d, i)) for d in range(dp_n) for i in range(ctx_n)]
    relay = [
        (d * ctx_n + i, d * ctx_n + (i + (1 if i & 1 else -1)) % ctx_n)
        for d in range(dp_n)
        for i in range(ctx_n)
    ]
    within = [
        (d * ctx_n + i, d * ctx_n + (i ^ 1)) for d in range(dp_n) for i in range(ctx_n)
    ]

    def trade(chunks, route):
        return [lax.ppermute(x, ("dp", "ctx"), route) for x in chunks]

    p_n, x_n = 1, 2
    mine_p = gate_product(me, k, v, grad, q, p_n, 1)
    got_p = trade(mine_p, across)
    mine_p, me = lax.optimization_barrier((mine_p, me))
    mine_x = gate_product(me, grad, q, k, v, x_n, 10**9)
    got_x = [jnp.concatenate(trade(mine_x, within), axis=1)]
    got_x, me = lax.optimization_barrier((got_x, me))
    got2_p = trade(got_x, relay)
    ahead, back = toeplitz(me, last, reaches, filters)
    ahead, me = lax.optimization_barrier((ahead, me))
    inside, weight = taps_inside(scale, me, reaches, mine_p[0], mine_x, got_x[0])
    local = taps(last, me, inside, weight, mine_p[0], got_p[0], got_x[0])
    local, got_p = lax.optimization_barrier((local, got_p))
    got2_x = trade(got_p, within)

    def trade_ctx(x, mask):
        return x + lax.ppermute(x, "ctx", [(i, i ^ mask) for i in range(ctx_n)])

    def trade_dp(x, mask):
        route = [
            (d * ctx_n + i, (d ^ mask) * ctx_n + (i ^ 1)) for d in range(dp_n) for i in range(ctx_n)
        ]
        return x + lax.ppermute(x, ("dp", "ctx"), route)

    total = trade_dp(local, 1)
    total = trade_dp(total, 3)
    total = trade_ctx(total, 1)
    total = trade_ctx(total, 8 | 1)
    outs = None
    fields = (mine_p, mine_x, got_p, got_x, got2_p, got2_x)
    pieces = 4
    for at, mask in enumerate((16 | 1, 56 | 1, 2 | 1, 6 | 1)):
        total, fields = lax.optimization_barrier((total, fields))
        outs = grads_piece(
            me, ahead, back, fields, (grad, k, v), outs,
            at * group_n // pieces, group_n // pieces, 2,
        )
        total = trade_ctx(total, mask)
        total, outs = lax.optimization_barrier((total, outs))
    shaped = [x.reshape(batch_n, tok_n, chan_n) for x in outs]
    return (*shaped, total)


def solution(mesh):
    block = P("dp", "ctx", None)
    return jax.shard_map(
        body,
        mesh=mesh,
        in_specs=(block, block, block, block, P(), P()),
        out_specs=(block, block, block, P()),
        check_vma=False,
    )
```

```python
import math

import jax
import jax.numpy as jnp
from jax import lax
from jax.experimental import pallas as pl
from jax.experimental.pallas import tpu as pltpu
from jax.sharding import PartitionSpec as P

F32 = jnp.float32
BF16 = jnp.bfloat16
TOK = 128
GW = 256


def whole():
    return pl.BlockSpec(memory_space=pltpu.VMEM)


def smem():
    return pl.BlockSpec(memory_space=pltpu.SMEM)


def params(mib):
    return pltpu.CompilerParams(vmem_limit_bytes=mib * 2**20)


def gate_product(me, a, b, c, d, chunks, flops):
    tok_n, chan_n = a.shape
    parts = 4
    rows = tok_n // parts
    width = chan_n // chunks

    def kernel(me_ref, a_ref, b_ref, c_ref, d_ref, *refs):
        outs, (left, right, sems) = refs[:chunks], refs[chunks:]

        def run(x_ref, y_ref):
            copies = []
            for i in range(parts):
                at = pl.ds(i * rows, rows)
                pair = (
                    pltpu.make_async_copy(x_ref.at[at], left.at[at], sems.at[0, i]),
                    pltpu.make_async_copy(y_ref.at[at], right.at[at], sems.at[1, i]),
                )
                for copy in pair:
                    copy.start()
                copies.append(pair)
            for i, pair in enumerate(copies):
                for copy in pair:
                    copy.wait()
                at = pl.ds(i * rows, rows)
                for j, out in enumerate(outs):
                    cols = pl.ds(j * width, width)
                    prod = left[at, cols].astype(F32) * right[at, cols].astype(F32)
                    out[at, :] = prod.astype(BF16)

        odd = (me_ref[0] & 1) == 1

        @pl.when(odd)
        def _():
            run(a_ref, b_ref)

        @pl.when(jnp.logical_not(odd))
        def _():
            run(c_ref, d_ref)

    fixed = (pltpu.with_memory_space_constraint(x, pltpu.HBM) for x in (a, b, c, d))
    return pl.pallas_call(
        kernel,
        out_shape=[jax.ShapeDtypeStruct((tok_n, width), BF16)] * chunks,
        in_specs=[smem()] + [pl.BlockSpec(memory_space=pltpu.HBM)] * 4,
        out_specs=[whole()] * chunks,
        scratch_shapes=[
            pltpu.VMEM((tok_n, chan_n), BF16),
            pltpu.VMEM((tok_n, chan_n), BF16),
            pltpu.SemaphoreType.DMA((2, parts)),
        ],
        compiler_params=params(8),
        cost_estimate=pl.CostEstimate(flops=flops, bytes_accessed=6 * a.size, transcendentals=0),
    )(me, *fixed)


def columns(chunks, g):
    at = g * GW
    for chunk in chunks:
        if at < chunk.shape[1]:
            return chunk[:, at : at + GW]
        at -= chunk.shape[1]


def toeplitz(me, last, reaches, filters):
    group_n = filters.shape[0]
    shape = jax.ShapeDtypeStruct((group_n, TOK, 3 * TOK), BF16)

    def kernel(me_ref, reach_ref, filt_ref, ahead_ref, back_ref):
        row = lax.broadcasted_iota(jnp.int32, (TOK, TOK), 0)
        col = lax.broadcasted_iota(jnp.int32, (TOK, TOK), 1)
        upper = col >= row
        lag = lax.broadcasted_iota(jnp.int32, (1, 2 * TOK), 1)
        here = me_ref[0]
        back1, back2 = (here > 0).astype(F32), (here > 1).astype(F32)
        ahead1, ahead2 = (here < last).astype(F32), (here < last - 1).astype(F32)
        zero = jnp.zeros((TOK, TOK), F32)
        lines = filt_ref[...].astype(F32)
        for g in range(group_n):
            line = jnp.where(lag < reach_ref[g], lines[g : g + 1, :], 0.0)
            near, far = (
                pltpu.roll(
                    jnp.broadcast_to(part, (TOK, TOK)), 0, axis=1, stride=1, stride_axis=0
                )
                for part in (line[:, :TOK], line[:, TOK:])
            )
            w0 = jnp.where(upper, near, zero)
            w1 = jnp.where(upper, far, near)
            w2 = jnp.where(upper, zero, far)
            ahead_ref[g, :, :TOK] = w0.astype(BF16)
            ahead_ref[g, :, TOK : 2 * TOK] = (w1 * ahead1).astype(BF16)
            ahead_ref[g, :, 2 * TOK :] = (w2 * ahead2).astype(BF16)
            back_ref[g, :, :TOK] = w0.T.astype(BF16)
            back_ref[g, :, TOK : 2 * TOK] = (w1 * back1).T.astype(BF16)
            back_ref[g, :, 2 * TOK :] = (w2 * back2).T.astype(BF16)

    return pl.pallas_call(
        kernel,
        out_shape=[shape, shape],
        in_specs=[smem(), smem(), whole()],
        out_specs=[whole(), whole()],
        compiler_params=params(8),
        cost_estimate=pl.CostEstimate(
            flops=group_n * TOK, bytes_accessed=group_n * TOK, transcendentals=0
        ),
    )(me, reaches, filters)


def tile_sums(upper, tile):
    sub = lax.broadcasted_iota(jnp.int32, (8, TOK), 0)
    acc = tile[0:8, :]
    for k in range(1, TOK // 8):
        acc = acc + pltpu.roll(tile[8 * k : 8 * k + 8, :], TOK - 8 * k, axis=1)
    for bit in (1, 2, 4):
        acc = jnp.where((sub & bit) != 0, pltpu.roll(acc, TOK - bit, axis=1), acc)
    return jnp.sum(acc, axis=0, keepdims=True)


def upper_mask():
    row = lax.broadcasted_iota(jnp.int32, (TOK, TOK), 0)
    col = lax.broadcasted_iota(jnp.int32, (TOK, TOK), 1)
    return col >= row


def cross(a, b):
    return lax.dot_general(a, b, (((1,), (1,)), ((), ())), preferred_element_type=F32)


def taps_inside(scale, me, reaches, mine_p, mine_x, got_x):
    group_n = mine_p.shape[1] // GW
    x_n = len(mine_x)

    def kernel(me_ref, reach_ref, mine_p, got_x, *refs):
        mine_x, out_ref, weight_ref = refs[:x_n], refs[x_n], refs[x_n + 1]
        upper = upper_mask()
        lag = lax.broadcasted_iota(jnp.int32, (1, 2 * TOK), 1)
        for g in range(group_n):
            weight_ref[g : g + 1, :] = jnp.where(lag < reach_ref[g], scale, 0.0).astype(F32)

        @pl.when((me_ref[0] & 1) == 1)
        def _():
            for g in range(group_n):
                dcv = columns(mine_x, g)
                c0 = cross(columns([mine_p], g), dcv)
                c1 = cross(columns([got_x], g), dcv)
                out_ref[g : g + 1, :TOK] = tile_sums(upper, jnp.where(upper, c0, c1))
                out_ref[g : g + 1, TOK:] = tile_sums(upper, jnp.where(upper, c1, 0.0))

        @pl.when((me_ref[0] & 1) == 0)
        def _():
            for g in range(group_n):
                c0 = cross(columns(mine_x, g), columns([mine_p], g))
                out_ref[g : g + 1, :TOK] = tile_sums(upper, jnp.where(upper, c0, 0.0))
            out_ref[:, TOK:] = jnp.zeros((group_n, TOK), F32)

    return pl.pallas_call(
        kernel,
        out_shape=[jax.ShapeDtypeStruct((group_n, 2 * TOK), F32)] * 2,
        in_specs=[smem(), smem()] + [whole()] * (2 + x_n),
        out_specs=[whole(), whole()],
        compiler_params=params(8),
        cost_estimate=pl.CostEstimate(
            flops=group_n * TOK, bytes_accessed=group_n * TOK, transcendentals=0
        ),
    )(me, reaches, mine_p, got_x, *mine_x)


def taps(last, me, inside, weight, mine_p, got_p, got_x):
    group_n = inside.shape[0]
    half = group_n // 2

    def kernel(me_ref, in_ref, weight_ref, mine_p, got_p, got_x, out_ref):
        upper = upper_mask()
        here = me_ref[0]
        odd = (here & 1) == 1

        def at(ref, g):
            return columns([ref], g)

        def work(near, far, near_groups, ok):
            for g in range(group_n):
                c2 = cross(*far(g))
                if g in near_groups:
                    c1 = cross(*near(g))
                    out_ref[g : g + 1, :TOK] = tile_sums(upper, jnp.where(upper, 0.0, c1))
                    out_ref[g : g + 1, TOK:] = tile_sums(upper, jnp.where(upper, c1, c2))
                else:
                    out_ref[g : g + 1, TOK:] = tile_sums(upper, jnp.where(upper, 0.0, c2))
            none = slice(half, group_n) if 0 in near_groups else slice(0, half)
            out_ref[none, :TOK] = jnp.zeros((half, TOK), F32)
            out_ref[...] = (in_ref[...] + jnp.where(ok, out_ref[...], 0.0)) * weight_ref[...]

        @pl.when(odd)
        def _():
            work(
                lambda g: (at(mine_p, g), at(got_p, g)),
                lambda g: (at(got_x, g), at(got_p, g)),
                range(half, group_n),
                here < last,
            )

        @pl.when(jnp.logical_not(odd))
        def _():
            work(
                lambda g: (at(got_p, g), at(mine_p, g)),
                lambda g: (at(got_p, g), at(got_x, g)),
                range(half),
                here > 0,
            )

    return pl.pallas_call(
        kernel,
        out_shape=jax.ShapeDtypeStruct((group_n, 2 * TOK), F32),
        in_specs=[smem()] + [whole()] * 5,
        out_specs=whole(),
        compiler_params=params(8),
        cost_estimate=pl.CostEstimate(
            flops=group_n * TOK, bytes_accessed=group_n * TOK, transcendentals=0
        ),
    )(me, inside, weight, mine_p, got_p, got_x)


def grads_piece(me, ahead, back, fields, gates, outs, first, count, step):
    tok_n, chan_n = gates[0].shape
    group_n = chan_n // GW
    start = first // step
    each = [group_n // len(x) for x in fields]
    fields = [x[first // n] for x, n in zip(fields, each)]
    cols = pl.BlockSpec((tok_n, step * GW), lambda i: (0, i + start))

    def kernel(me_ref, ahead_ref, back_ref, *refs):
        grad, kpart, vpart = refs[6:9]
        gq, gk, gv = refs[-3:]
        base = first + pl.program_id(0) * step

        def dot(a, b):
            return jnp.dot(a, b, preferred_element_type=F32)

        def cols_of(ref, offset, g):
            return ref[:, pl.ds(pl.multiple_of((base - offset + g) * GW, GW), GW)]

        def work(*order):
            for g in range(step):
                at = slice(g * GW, (g + 1) * GW)
                src = pl.ds(pl.multiple_of((base + g) * GW, GW), GW)
                sig, sig1, sig2, dcv, dcv1, dcv2 = (
                    cols_of(refs[i], first - first % each[i], g) for i in order
                )
                conv = dot(back_ref[base + g], jnp.concatenate([sig, sig1, sig2], axis=0))
                gq[:, at] = (grad[:, src].astype(F32) * conv).astype(BF16)
                dsig = dot(ahead_ref[base + g], jnp.concatenate([dcv, dcv1, dcv2], axis=0))
                gk[:, at] = (dsig * vpart[:, src].astype(F32)).astype(BF16)
                gv[:, at] = (dsig * kpart[:, src].astype(F32)).astype(BF16)

        odd = (me_ref[0] & 1) == 1

        @pl.when(odd)
        def _():
            work(0, 3, 5, 1, 2, 4)

        @pl.when(jnp.logical_not(odd))
        def _():
            work(1, 2, 4, 0, 3, 5)

    shape = jax.ShapeDtypeStruct((tok_n, chan_n), BF16)
    earlier = [] if outs is None else list(outs)
    part = count * TOK * GW
    return pl.pallas_call(
        kernel,
        out_shape=[shape] * 3,
        grid=(count // step,),
        in_specs=[smem()] + [whole()] * 11 + [pl.BlockSpec(memory_space=pl.ANY)] * len(earlier),
        out_specs=[cols] * 3,
        input_output_aliases={12 + i: i for i in range(len(earlier))},
        compiler_params=params(8),
        cost_estimate=pl.CostEstimate(
            flops=12 * part * TOK, bytes_accessed=27 * part, transcendentals=0
        ),
    )(me, ahead, back, *fields, *gates, *earlier)


def body(q_proj, k_proj, v_proj, out_grad, filters, reaches):
    batch_n, tok_n, chan_n = q_proj.shape
    group_n = filters.shape[0]
    ctx_n, dp_n = lax.axis_size("ctx"), lax.axis_size("dp")
    scale = 1.0 / math.sqrt(batch_n * dp_n * tok_n * ctx_n * (chan_n // group_n))
    q, k, v, grad = (x.reshape(tok_n, chan_n) for x in (q_proj, k_proj, v_proj, out_grad))

    me = lax.axis_index("ctx").astype(jnp.int32)[None]
    last = ctx_n - 1

    def partner(d, i):
        if i in (0, last):
            return (d ^ 1) * ctx_n + i
        return d * ctx_n + (i + 1 if i & 1 else i - 1)

    across = [(d * ctx_n + i, partner(d, i)) for d in range(dp_n) for i in range(ctx_n)]
    relay = [
        (d * ctx_n + i, d * ctx_n + (i + (1 if i & 1 else -1)) % ctx_n)
        for d in range(dp_n)
        for i in range(ctx_n)
    ]
    within = [
        (d * ctx_n + i, d * ctx_n + (i ^ 1)) for d in range(dp_n) for i in range(ctx_n)
    ]

    def trade(chunks, route):
        return [lax.ppermute(x, ("dp", "ctx"), route) for x in chunks]

    p_n, x_n = 1, 2
    mine_p = gate_product(me, k, v, grad, q, p_n, 1)
    got_p = trade(mine_p, across)
    mine_p, me = lax.optimization_barrier((mine_p, me))
    mine_x = gate_product(me, grad, q, k, v, x_n, 10**9)
    got_x = [jnp.concatenate(trade(mine_x, within), axis=1)]
    got_x, me = lax.optimization_barrier((got_x, me))
    got2_p = trade(got_x, relay)
    ahead, back = toeplitz(me, last, reaches, filters)
    ahead, me = lax.optimization_barrier((ahead, me))
    inside, weight = taps_inside(scale, me, reaches, mine_p[0], mine_x, got_x[0])
    local = taps(last, me, inside, weight, mine_p[0], got_p[0], got_x[0])
    local, got_p = lax.optimization_barrier((local, got_p))
    got2_x = trade(got_p, within)

    def trade_ctx(x, mask):
        return x + lax.ppermute(x, "ctx", [(i, i ^ mask) for i in range(ctx_n)])

    def trade_dp(x, mask):
        route = [
            (d * ctx_n + i, (d ^ mask) * ctx_n + (i ^ 1)) for d in range(dp_n) for i in range(ctx_n)
        ]
        return x + lax.ppermute(x, ("dp", "ctx"), route)

    total = trade_dp(local, 1)
    total = trade_dp(total, 3)
    total = trade_ctx(total, 1)
    total = trade_ctx(total, 8 | 1)
    outs = None
    fields = (mine_p, mine_x, got_p, got_x, got2_p, got2_x)
    pieces = 4
    for at, mask in enumerate((16 | 1, 56 | 1, 2 | 1, 6)):
        total, fields = lax.optimization_barrier((total, fields))
        outs = grads_piece(
            me, ahead, back, fields, (grad, k, v), outs,
            at * group_n // pieces, group_n // pieces, 2,
        )
        total = trade_ctx(total, mask)
        total, outs = lax.optimization_barrier((total, outs))
    shaped = [x.reshape(batch_n, tok_n, chan_n) for x in outs]
    return (*shaped, total)


def solution(mesh):
    block = P("dp", "ctx", None)
    return jax.shard_map(
        body,
        mesh=mesh,
        in_specs=(block, block, block, block, P(), P()),
        out_specs=(block, block, block, P()),
        check_vma=False,
    )
```

```python
import math

import jax
import jax.numpy as jnp
from jax import lax
from jax.experimental import pallas as pl
from jax.experimental.pallas import tpu as pltpu
from jax.sharding import PartitionSpec as P

F32 = jnp.float32
BF16 = jnp.bfloat16
TOK = 128
GW = 256


def whole():
    return pl.BlockSpec(memory_space=pltpu.VMEM)


def smem():
    return pl.BlockSpec(memory_space=pltpu.SMEM)


def params(mib):
    return pltpu.CompilerParams(vmem_limit_bytes=mib * 2**20)


def gate_product(me, a, b, c, d, chunks, flops):
    tok_n, chan_n = a.shape
    parts = 4
    rows = tok_n // parts
    width = chan_n // chunks

    def kernel(me_ref, a_ref, b_ref, c_ref, d_ref, *refs):
        outs, (left, right, sems) = refs[:chunks], refs[chunks:]

        def run(x_ref, y_ref):
            copies = []
            for i in range(parts):
                at = pl.ds(i * rows, rows)
                pair = (
                    pltpu.make_async_copy(x_ref.at[at], left.at[at], sems.at[0, i]),
                    pltpu.make_async_copy(y_ref.at[at], right.at[at], sems.at[1, i]),
                )
                for copy in pair:
                    copy.start()
                copies.append(pair)
            for i, pair in enumerate(copies):
                for copy in pair:
                    copy.wait()
                at = pl.ds(i * rows, rows)
                for j, out in enumerate(outs):
                    cols = pl.ds(j * width, width)
                    prod = left[at, cols].astype(F32) * right[at, cols].astype(F32)
                    out[at, :] = prod.astype(BF16)

        odd = (me_ref[0] & 1) == 1

        @pl.when(odd)
        def _():
            run(a_ref, b_ref)

        @pl.when(jnp.logical_not(odd))
        def _():
            run(c_ref, d_ref)

    fixed = (pltpu.with_memory_space_constraint(x, pltpu.HBM) for x in (a, b, c, d))
    return pl.pallas_call(
        kernel,
        out_shape=[jax.ShapeDtypeStruct((tok_n, width), BF16)] * chunks,
        in_specs=[smem()] + [pl.BlockSpec(memory_space=pltpu.HBM)] * 4,
        out_specs=[whole()] * chunks,
        scratch_shapes=[
            pltpu.VMEM((tok_n, chan_n), BF16),
            pltpu.VMEM((tok_n, chan_n), BF16),
            pltpu.SemaphoreType.DMA((2, parts)),
        ],
        compiler_params=params(8),
        cost_estimate=pl.CostEstimate(flops=flops, bytes_accessed=6 * a.size, transcendentals=0),
    )(me, *fixed)


def columns(chunks, g):
    at = g * GW
    for chunk in chunks:
        if at < chunk.shape[1]:
            return chunk[:, at : at + GW]
        at -= chunk.shape[1]


def toeplitz(me, last, reaches, filters):
    group_n = filters.shape[0]
    shape = jax.ShapeDtypeStruct((group_n, TOK, 3 * TOK), BF16)

    def kernel(me_ref, reach_ref, filt_ref, ahead_ref, back_ref):
        row = lax.broadcasted_iota(jnp.int32, (TOK, TOK), 0)
        col = lax.broadcasted_iota(jnp.int32, (TOK, TOK), 1)
        upper = col >= row
        lag = lax.broadcasted_iota(jnp.int32, (1, 2 * TOK), 1)
        here = me_ref[0]
        back1, back2 = (here > 0).astype(F32), (here > 1).astype(F32)
        ahead1, ahead2 = (here < last).astype(F32), (here < last - 1).astype(F32)
        zero = jnp.zeros((TOK, TOK), F32)
        lines = filt_ref[...].astype(F32)
        for g in range(group_n):
            line = jnp.where(lag < reach_ref[g], lines[g : g + 1, :], 0.0)
            near, far = (
                pltpu.roll(
                    jnp.broadcast_to(part, (TOK, TOK)), 0, axis=1, stride=1, stride_axis=0
                )
                for part in (line[:, :TOK], line[:, TOK:])
            )
            w0 = jnp.where(upper, near, zero)
            w1 = jnp.where(upper, far, near)
            w2 = jnp.where(upper, zero, far)
            ahead_ref[g, :, :TOK] = w0.astype(BF16)
            ahead_ref[g, :, TOK : 2 * TOK] = (w1 * ahead1).astype(BF16)
            ahead_ref[g, :, 2 * TOK :] = (w2 * ahead2).astype(BF16)
            back_ref[g, :, :TOK] = w0.T.astype(BF16)
            back_ref[g, :, TOK : 2 * TOK] = (w1 * back1).T.astype(BF16)
            back_ref[g, :, 2 * TOK :] = (w2 * back2).T.astype(BF16)

    return pl.pallas_call(
        kernel,
        out_shape=[shape, shape],
        in_specs=[smem(), smem(), whole()],
        out_specs=[whole(), whole()],
        compiler_params=params(8),
        cost_estimate=pl.CostEstimate(
            flops=group_n * TOK, bytes_accessed=group_n * TOK, transcendentals=0
        ),
    )(me, reaches, filters)


def tile_sums(upper, tile):
    sub = lax.broadcasted_iota(jnp.int32, (8, TOK), 0)
    acc = tile[0:8, :]
    for k in range(1, TOK // 8):
        acc = acc + pltpu.roll(tile[8 * k : 8 * k + 8, :], TOK - 8 * k, axis=1)
    for bit in (1, 2, 4):
        acc = jnp.where((sub & bit) != 0, pltpu.roll(acc, TOK - bit, axis=1), acc)
    return jnp.sum(acc, axis=0, keepdims=True)


def upper_mask():
    row = lax.broadcasted_iota(jnp.int32, (TOK, TOK), 0)
    col = lax.broadcasted_iota(jnp.int32, (TOK, TOK), 1)
    return col >= row


def cross(a, b):
    return lax.dot_general(a, b, (((1,), (1,)), ((), ())), preferred_element_type=F32)


def taps_inside(scale, me, reaches, mine_p, mine_x, got_x):
    group_n = mine_p.shape[1] // GW
    x_n = len(mine_x)

    def kernel(me_ref, reach_ref, mine_p, got_x, *refs):
        mine_x, out_ref, weight_ref = refs[:x_n], refs[x_n], refs[x_n + 1]
        upper = upper_mask()
        lag = lax.broadcasted_iota(jnp.int32, (1, 2 * TOK), 1)
        for g in range(group_n):
            weight_ref[g : g + 1, :] = jnp.where(lag < reach_ref[g], scale, 0.0).astype(F32)

        @pl.when((me_ref[0] & 1) == 1)
        def _():
            for g in range(group_n):
                dcv = columns(mine_x, g)
                c0 = cross(columns([mine_p], g), dcv)
                c1 = cross(columns([got_x], g), dcv)
                out_ref[g : g + 1, :TOK] = tile_sums(upper, jnp.where(upper, c0, c1))
                out_ref[g : g + 1, TOK:] = tile_sums(upper, jnp.where(upper, c1, 0.0))

        @pl.when((me_ref[0] & 1) == 0)
        def _():
            for g in range(group_n):
                c0 = cross(columns(mine_x, g), columns([mine_p], g))
                out_ref[g : g + 1, :TOK] = tile_sums(upper, jnp.where(upper, c0, 0.0))
            out_ref[:, TOK:] = jnp.zeros((group_n, TOK), F32)

    return pl.pallas_call(
        kernel,
        out_shape=[jax.ShapeDtypeStruct((group_n, 2 * TOK), F32)] * 2,
        in_specs=[smem(), smem()] + [whole()] * (2 + x_n),
        out_specs=[whole(), whole()],
        compiler_params=params(8),
        cost_estimate=pl.CostEstimate(
            flops=group_n * TOK, bytes_accessed=group_n * TOK, transcendentals=0
        ),
    )(me, reaches, mine_p, got_x, *mine_x)


def taps(last, me, inside, weight, mine_p, got_p, got_x):
    group_n = inside.shape[0]
    half = group_n // 2

    def kernel(me_ref, in_ref, weight_ref, mine_p, got_p, got_x, out_ref):
        upper = upper_mask()
        here = me_ref[0]
        odd = (here & 1) == 1

        def at(ref, g):
            return columns([ref], g)

        def work(near, far, near_groups, ok):
            for g in range(group_n):
                c2 = cross(*far(g))
                if g in near_groups:
                    c1 = cross(*near(g))
                    out_ref[g : g + 1, :TOK] = tile_sums(upper, jnp.where(upper, 0.0, c1))
                    out_ref[g : g + 1, TOK:] = tile_sums(upper, jnp.where(upper, c1, c2))
                else:
                    out_ref[g : g + 1, TOK:] = tile_sums(upper, jnp.where(upper, 0.0, c2))
            none = slice(half, group_n) if 0 in near_groups else slice(0, half)
            out_ref[none, :TOK] = jnp.zeros((half, TOK), F32)
            out_ref[...] = (in_ref[...] + jnp.where(ok, out_ref[...], 0.0)) * weight_ref[...]

        @pl.when(odd)
        def _():
            work(
                lambda g: (at(mine_p, g), at(got_p, g)),
                lambda g: (at(got_x, g), at(got_p, g)),
                range(half, group_n),
                here < last,
            )

        @pl.when(jnp.logical_not(odd))
        def _():
            work(
                lambda g: (at(got_p, g), at(mine_p, g)),
                lambda g: (at(got_p, g), at(got_x, g)),
                range(half),
                here > 0,
            )

    return pl.pallas_call(
        kernel,
        out_shape=jax.ShapeDtypeStruct((group_n, 2 * TOK), F32),
        in_specs=[smem()] + [whole()] * 5,
        out_specs=whole(),
        compiler_params=params(8),
        cost_estimate=pl.CostEstimate(
            flops=group_n * TOK, bytes_accessed=group_n * TOK, transcendentals=0
        ),
    )(me, inside, weight, mine_p, got_p, got_x)


def grads_piece(me, ahead, back, fields, gates, outs, first, count, step):
    tok_n, chan_n = gates[0].shape
    group_n = chan_n // GW
    start = first // step
    each = [group_n // len(x) for x in fields]
    fields = [x[first // n] for x, n in zip(fields, each)]
    cols = pl.BlockSpec((tok_n, step * GW), lambda i: (0, i + start))

    def kernel(me_ref, ahead_ref, back_ref, *refs):
        grad, kpart, vpart = refs[6:9]
        gq, gk, gv = refs[-3:]
        base = first + pl.program_id(0) * step

        def dot(a, b):
            return jnp.dot(a, b, preferred_element_type=F32)

        def cols_of(ref, offset, g):
            return ref[:, pl.ds(pl.multiple_of((base - offset + g) * GW, GW), GW)]

        def work(*order):
            for g in range(step):
                at = slice(g * GW, (g + 1) * GW)
                src = pl.ds(pl.multiple_of((base + g) * GW, GW), GW)
                sig, sig1, sig2, dcv, dcv1, dcv2 = (
                    cols_of(refs[i], first - first % each[i], g) for i in order
                )
                conv = dot(back_ref[base + g], jnp.concatenate([sig, sig1, sig2], axis=0))
                gq[:, at] = (grad[:, src].astype(F32) * conv).astype(BF16)
                dsig = dot(ahead_ref[base + g], jnp.concatenate([dcv, dcv1, dcv2], axis=0))
                gk[:, at] = (dsig * vpart[:, src].astype(F32)).astype(BF16)
                gv[:, at] = (dsig * kpart[:, src].astype(F32)).astype(BF16)

        odd = (me_ref[0] & 1) == 1

        @pl.when(odd)
        def _():
            work(0, 3, 5, 1, 2, 4)

        @pl.when(jnp.logical_not(odd))
        def _():
            work(1, 2, 4, 0, 3, 5)

    shape = jax.ShapeDtypeStruct((tok_n, chan_n), BF16)
    earlier = [] if outs is None else list(outs)
    part = count * TOK * GW
    return pl.pallas_call(
        kernel,
        out_shape=[shape] * 3,
        grid=(count // step,),
        in_specs=[smem()] + [whole()] * 11 + [pl.BlockSpec(memory_space=pl.ANY)] * len(earlier),
        out_specs=[cols] * 3,
        input_output_aliases={12 + i: i for i in range(len(earlier))},
        compiler_params=params(8),
        cost_estimate=pl.CostEstimate(
            flops=12 * part * TOK, bytes_accessed=27 * part, transcendentals=0
        ),
    )(me, ahead, back, *fields, *gates, *earlier)


def body(q_proj, k_proj, v_proj, out_grad, filters, reaches):
    batch_n, tok_n, chan_n = q_proj.shape
    group_n = filters.shape[0]
    ctx_n, dp_n = lax.axis_size("ctx"), lax.axis_size("dp")
    scale = 1.0 / math.sqrt(batch_n * dp_n * tok_n * ctx_n * (chan_n // group_n))
    q, k, v, grad = (x.reshape(tok_n, chan_n) for x in (q_proj, k_proj, v_proj, out_grad))

    me = lax.axis_index("ctx").astype(jnp.int32)[None]
    last = ctx_n - 1

    def partner(d, i):
        if i in (0, last):
            return (d ^ 1) * ctx_n + i
        return d * ctx_n + (i + 1 if i & 1 else i - 1)

    across = [(d * ctx_n + i, partner(d, i)) for d in range(dp_n) for i in range(ctx_n)]
    relay = [
        (d * ctx_n + i, d * ctx_n + (i + (1 if i & 1 else -1)) % ctx_n)
        for d in range(dp_n)
        for i in range(ctx_n)
    ]
    within = [
        (d * ctx_n + i, d * ctx_n + (i ^ 1)) for d in range(dp_n) for i in range(ctx_n)
    ]

    def trade(chunks, route):
        return [lax.ppermute(x, ("dp", "ctx"), route) for x in chunks]

    p_n, x_n = 1, 2
    mine_p = gate_product(me, k, v, grad, q, p_n, 1)
    got_p = trade(mine_p, across)
    mine_p, me = lax.optimization_barrier((mine_p, me))
    mine_x = gate_product(me, grad, q, k, v, x_n, 10**9)
    got_x = [jnp.concatenate(trade(mine_x, within), axis=1)]
    got_x, me = lax.optimization_barrier((got_x, me))
    got2_p = trade(got_x, relay)
    ahead, back = toeplitz(me, last, reaches, filters)
    ahead, me = lax.optimization_barrier((ahead, me))
    inside, weight = taps_inside(scale, me, reaches, mine_p[0], mine_x, got_x[0])
    local = taps(last, me, inside, weight, mine_p[0], got_p[0], got_x[0])
    local, got_p = lax.optimization_barrier((local, got_p))
    got2_x = trade(got_p, within)

    def trade_ctx(x, mask):
        return x + lax.ppermute(x, "ctx", [(i, i ^ mask) for i in range(ctx_n)])

    def trade_dp(x, mask):
        route = [
            (d * ctx_n + i, (d ^ mask) * ctx_n + (i ^ 1)) for d in range(dp_n) for i in range(ctx_n)
        ]
        return x + lax.ppermute(x, ("dp", "ctx"), route)

    total = trade_dp(local, 3)
    total = trade_dp(total, 1)
    total = trade_ctx(total, 1)
    total = trade_ctx(total, 8 | 1)
    outs = None
    fields = (mine_p, mine_x, got_p, got_x, got2_p, got2_x)
    pieces = 4
    for at, mask in enumerate((16 | 1, 56 | 1, 6, 2 | 1)):
        total, fields = lax.optimization_barrier((total, fields))
        outs = grads_piece(
            me, ahead, back, fields, (grad, k, v), outs,
            at * group_n // pieces, group_n // pieces, 2,
        )
        total = trade_ctx(total, mask)
        total, outs = lax.optimization_barrier((total, outs))
    shaped = [x.reshape(batch_n, tok_n, chan_n) for x in outs]
    return (*shaped, total)


def solution(mesh):
    block = P("dp", "ctx", None)
    return jax.shard_map(
        body,
        mesh=mesh,
        in_specs=(block, block, block, block, P(), P()),
        out_specs=(block, block, block, P()),
        check_vma=False,
    )
```
